512 devices in a mesh: row: 32 (over z_lo, y), col: 16 (over z_hi, x, core).
Axes of the slice: x: 4, y: 8, z: 8 (z_hi: 2, z_lo: 4; z = z_hi * 4 + z_lo), core: 2. Of those that a mesh axis runs over, the one named last changes fastest.
Arguments:
- center: bfloat16 [2048, 8192], P('col', 'row'), may hold values from -6 to 6
- radius: bfloat16 [2048, 8192], P('col', 'row'), may hold values from 0.049804688 to 1
- grad_center: bfloat16 [2048, 8192], P('row', 'col'), may hold values from -6 to 6
- grad_radius: bfloat16 [2048, 8192], P('row', 'col'), may hold values from -6 to 6
- weight: bfloat16 [8192, 8192], P('row', 'col'), may hold values from -0.0625 to 0.0625
- active: int32 [2048, 8192], P('col', 'row'), may hold values 0 or 1
Outputs:
- center_in: float32 [2048, 8192], P('col', 'row')
- radius_in: float32 [2048, 8192], P('col', 'row')
- weight_grad: float32 [8192, 8192], P('row', 'col')
The draws below stay inside these ranges and needn't reach their ends.
All inputs are finite; a program needn't handle non-finite values. No bound on the sum of `active` on one device may be relied on, other than what follows from the above.
Results may differ from the reference program's by a relative error of at most 0.0003.
Values may be sent and summed in bfloat16 or wider, within the bound.
A program may use at most 64 MiB of HBM per device.

```python
import jax
import jax.numpy as jnp

D = 8192
INNER = 8192
TOK = 2048


def plant(array, rng, low, top_value):
    index_at = [jax.random.randint(jax.random.fold_in(rng, axis), (), 0, length) for axis, length in enumerate(array.shape)]
    widest = array.shape.index(max(array.shape))
    next_to = index_at[:widest] + [(index_at[widest] + 1) % array.shape[widest]] + index_at[widest + 1:]
    return array.at[tuple(index_at)].set(low).at[tuple(next_to)].set(top_value)


def spiked(drawn, key, source, target, shards_of, factor):
    def block_of(position):
        return (jnp.arange(drawn.shape[position]) // (drawn.shape[position] // shards_of)).reshape((-1,) + (1,) * (drawn.ndim - 1 - position))

    first = jax.random.permutation(key, shards_of)[block_of(target)]
    far = (block_of(target) + shards_of // 2) % shards_of
    return jnp.where((block_of(source) == first) | (block_of(source) == far), factor * drawn, drawn)


def shard_levels(own_key, extent, split, smallest, largest):
    def one(dim, parts):
        draws = jax.random.uniform(jax.random.fold_in(jax.random.fold_in(own_key, 6), dim), (parts,), jnp.float32, smallest / len(split), largest / len(split))
        return jnp.repeat(jnp.exp(draws), extent[dim] // parts).reshape((-1,) + (1,) * (len(extent) - dim - 1))

    loudness = one(*split[0])
    for cut in split[1:]:
        loudness = loudness * one(*cut)
    return loudness


def scatter_about(key, extent, scale, most, split=(), dtype=jnp.bfloat16):
    drawn = jax.random.normal(key, extent, jnp.float32) * scale
    if len(split) > 0:
        drawn = shard_levels(key, extent, split, -0.22, 0.18) * drawn
    return jnp.clip(drawn, min=-most, max=most).astype(dtype)


def bell_draw_with(stream_key, dims, scale, bound, cuts, heavy, kind=jnp.bfloat16):
    drawn = scale * jax.random.normal(stream_key, dims, jnp.float32)
    if cuts:
        drawn = drawn * shard_levels(stream_key, dims, cuts, -0.22, 0.18)
    return jnp.clip(spiked(drawn, jax.random.fold_in(stream_key, 3), *heavy), -bound, bound).astype(kind)


def setup_inputs(seed: int = 0) -> dict:
    splits = jax.random.split(jax.random.key(seed), 7)
    return {
        "center": scatter_about(splits[0], (TOK, INNER), 1.0, 6.0, ((0, 16), (1, 32))),
        "radius": jnp.clip(0.049804688 + 0.9501953 * jax.random.uniform(splits[1], (TOK, INNER), jnp.float32) ** shard_levels(splits[1], (TOK, INNER), ((0, 16), (1, 32)), -0.2, 0.2), 0.049804688, 1.0).astype(jnp.bfloat16),
        "grad_center": bell_draw_with(splits[2], (TOK, D), 1.0, 6.0, ((0, 32), (1, 16)), (1, 0, 32, 2.75)),
        "grad_radius": bell_draw_with(splits[3], (TOK, D), 1.0, 6.0, ((0, 32), (1, 16)), (1, 0, 32, 2.75)),
        "weight": scatter_about(splits[4], (INNER, D), INNER ** -0.5, 0.0625, ((0, 32), (1, 16))),
        "active": plant((jax.random.randint(splits[5], (TOK, INNER), 0, 4) < 3).astype(jnp.int32), jax.random.fold_in(splits[5], 1), 0, 1),
    }


def reference(center, radius, grad_center, grad_radius, weight, active):
    magnitude = jnp.abs(weight)
    gating = active.astype(jnp.float32)
    center_sum = jnp.dot(grad_center, weight.T, preferred_element_type=jnp.float32)
    radius_sum = jnp.dot(grad_radius, magnitude.T, preferred_element_type=jnp.float32)
    center_in = gating * center_sum
    radius_in = gating * radius_sum
    center_part = jnp.dot(center.T, grad_center, preferred_element_type=jnp.float32)
    radius_part = jnp.dot(radius.T, grad_radius, preferred_element_type=jnp.float32)
    scale_factor = jnp.float32(1.0) / jnp.sqrt(jnp.float32(TOK))
    weight_grad = (center_part + jnp.sign(weight).astype(jnp.float32) * radius_part) * scale_factor
    return (center_in, radius_in, weight_grad)
```

```python
import functools

import jax
import jax.numpy as jnp
from jax import lax
from jax.experimental import pallas as pl
from jax.experimental.pallas import tpu as pltpu
from jax.sharding import PartitionSpec as P

MESH = pl.DeviceIdType.MESH
F32 = jnp.float32
BF16 = jnp.bfloat16


def dot_nt(a, b):
    return lax.dot_general(a, b, (((1,), (1,)), ((), ())), preferred_element_type=F32)


def dot_tn(a, b):
    return lax.dot_general(a, b, (((0,), (0,)), ((), ())), preferred_element_type=F32)


def kernel(
    scale,
    ctr, rad, gc, gr, w, act,
    oc, orad, ow,
    G, C, Wb, Wa, S, R, Zs, F, acc, wsend, wrecv,
    ring_s, ring_r, own_s, own_r, z_s, z_r, sib_s, sib_r, cin_s, cin_r, x_s, x_r, f_s, f_r,
):
    row, col = lax.axis_index("row"), lax.axis_index("col")
    zl, y = row // 8, row % 8
    zh, x, k = col // 8, (col % 8) // 2, col % 2
    z1, z0 = zl // 2, zl % 2
    mid = (z0 + z1) % 2

    def dev(x=x, y=y, zl=zl, zh=zh, k=k):
        return (zl * 8 + y, zh * 8 + x * 2 + k)

    def flip(j):
        return ((z1 + j // 2) % 2) * 2 + (z0 + j % 2) % 2

    order = [0, 1, 2 + mid, 3 - mid]
    ok = 1 - k
    up, down = (y + 1) % 8, (y + 7) % 8

    def rows32(i):
        return pl.ds(pl.multiple_of(i * 32, 32), 32)

    def at_y(off):
        return (y + off + 8) % 8

    sent = []

    def copy(src, dst, ssem, rsem, to):
        return pltpu.make_async_remote_copy(
            src_ref=src, dst_ref=dst, send_sem=ssem, recv_sem=rsem, device_id=to, device_id_type=MESH
        )

    def send(c, cond=None):
        if cond is None:
            c.start()
        else:
            pl.when(cond)(c.start)
        sent.append((c, cond))

    zrows = rows32(zl)
    G[y, 0, k, zrows] = gc[rows32(k)]
    G[y, 1, k, zrows] = gr[rows32(k)]
    cz = rows32(zh * 2 + x // 2)
    cy = (x % 2) * 4 + k * 2
    C[pl.ds(cy, 2), 0, cz] = ctr[:, rows32(k)]
    C[pl.ds(cy, 2), 1, cz] = rad[:, rows32(k)]

    peers = [dev(y=up), dev(y=down), dev(k=ok), dev(zh=1 - zh), dev(zh=1 - zh, k=ok)]
    peers += [dev(zl=flip(j)) for j in (1, 2, 3)]
    peers += [dev(x=(x + i) % 4) for i in (1, 2, 3)]
    bar = pltpu.get_barrier_semaphore()
    for p in peers:
        pl.semaphore_signal(bar, inc=1, device_id=p, device_id_type=MESH)
    pl.semaphore_wait(bar, len(peers))

    def own_y(part, kc):
        blk = G.at[y, :, kc, zrows]
        for i, to in enumerate((up, down)):
            send(copy(blk, blk, own_s.at[part, i], own_r.at[part, i], dev(y=to)))

    def own_z(part, kc):
        blk = G.at[y, :, kc, zrows]
        for i in (1, 2, 3):
            j = order[i]
            send(copy(blk, blk, z_s.at[part, i - 1], z_r.at[part, j - 1], dev(zl=flip(j))))

    own_y(0, k)
    sib = dev(k=ok)
    gsib = [copy(ref.at[rows32(ok)], G.at[y, a, k, zrows], sib_s.at[a], sib_r.at[a], sib) for a, ref in enumerate((gc, gr))]
    csib = [
        copy(ref.at[:, rows32(ok)], C.at[pl.ds(cy, 2), a, cz], sib_s.at[2 + a], sib_r.at[2 + a], sib)
        for a, ref in enumerate((ctr, rad))
    ]
    wsib = copy(w, Wb.at[k], sib_s.at[4], sib_r.at[4], sib)
    for c in gsib:
        send(c)
    own_z(0, k)
    for c in csib:
        send(c)
    send(wsib)
    Wb[k] = w[...]
    Wa[k] = jnp.abs(w[...])
    for c in gsib:
        c.wait_recv()
    own_y(1, ok)
    own_z(1, ok)
    for c in csib:
        c.wait_recv()

    def cin(zh_):
        return C.at[pl.ds((x % 2) * 4, 4), :, rows32(zh_ * 2 + x // 2)]

    def cin_x(zh_, part):
        for i in (1, 2, 3):
            blk = cin(zh_)
            send(copy(blk, blk, cin_s.at[part, i - 1], cin_r.at[part, i - 1], dev(x=(x + i) % 4)))

    far = copy(cin(zh), cin(zh), cin_s.at[2, 0], cin_r.at[2, 0], dev(zh=1 - zh))
    send(far)
    cin_x(zh, 0)

    def ring_copy(j, d, up_dir):
        ys = at_y(-d) if up_dir else at_y(d)
        i = 0 if up_dir else 1
        zr = rows32(flip(order[j]))
        if d < 3:
            blk = G.at[ys, :, :, zr]
        else:
            blk = G.at[ys, i, :, zr]
        return copy(blk, blk, ring_s.at[i, d, j], ring_r.at[i, d, j], dev(y=up if up_dir else down))

    def arrive(j, d):
        if d == 0:
            if j:
                jj = order[j]
                blk = G.at[y, :, k, zrows]
                for part in (0, 1):
                    copy(blk, blk, z_s.at[part, 0], z_r.at[part, jj - 1], dev()).wait_recv()
        elif d == 1 and j == 0:
            blk = G.at[y, :, k, zrows]
            for part in (0, 1):
                for i in (0, 1):
                    copy(blk, blk, own_s.at[part, i], own_r.at[part, i], dev()).wait_recv()
        else:
            ring_copy(j, d - 1, True).wait_recv()
            ring_copy(j, d - 1, False).wait_recv()

    def step(j, d):
        arrive(j, d)
        if d < 4:
            send(ring_copy(j, d, True))
            send(ring_copy(j, d, False))

    def x_copy(yb, g):
        xd = g * 2 + yb // 4
        return copy(S.at[yb, :, :, g], R.at[x, yb % 4], x_s.at[yb, g], x_r.at[x, yb % 4], dev(x=xd)), xd != x

    def through(off):
        yb = at_y(off)
        for a, m in ((0, Wb), (1, Wa)):
            p = dot_nt(G[yb, a, 0], m[0]) + dot_nt(G[yb, a, 1], m[1])
            S[yb, a] = p.reshape(2, 2, 32, 256)
        for g in (0, 1):
            c, cond = x_copy(yb, g)
            send(c, cond)

    def grad(off, first=False):
        yb = at_y(off)
        for a in (0, 1):
            for kc in (0, 1):
                t = dot_tn(C[yb, a], G[yb, a, kc])
                if first:
                    acc[a, kc] = t
                else:
                    acc[a, kc] += t

    def f_send(src, to, slot_s, slot_r):
        return copy(src, F.at[zh, k, slot_r], f_s.at[slot_s], f_r.at[zh, k, slot_r], to)

    def owner(off):
        yb = at_y(off)
        yq = yb % 4
        mine = yb // 4 == x % 2
        to_core, yy = yq // 2, yq % 2

        @pl.when(mine)
        def _():
            g = x // 2
            for i in (1, 2, 3):
                xs = (x + i) % 4
                copy(S.at[yb, :, :, g], R.at[xs, yq], x_s.at[yb, g], x_r.at[xs, yq], dev()).wait_recv()
            for a in (0, 1):
                for h in (zh, 1 - zh):
                    t = S[yb, a, h, g]
                    for i in (1, 2, 3):
                        t = t + R[(x + i) % 4, yq, a, h]
                    Zs[yq, h, a] = t

        send(f_send(Zs.at[yq, 1 - zh], dev(zh=1 - zh, k=to_core), yq, yy), mine)
        here = Zs.at[yq, zh]
        send(f_send(here, dev(k=ok), 4 + yy, yy), mine & (to_core != k))

        @pl.when(mine & (to_core == k))
        def _():
            F[zh, k, yy] = Zs[yq, zh]

    step(1, 0)
    step(0, 1)
    step(2, 0)
    step(3, 0)
    wsib.wait_recv()
    Wa[ok] = jnp.abs(Wb[ok])
    through(0)
    step(1, 1)
    far_in = copy(cin(1 - zh), cin(1 - zh), cin_s.at[2, 0], cin_r.at[2, 0], dev())
    far_in.wait_recv()
    cin_x(1 - zh, 1)
    step(2, 1)
    step(3, 1)
    through(1)
    through(-1)
    step(0, 2)
    owner(0)
    step(1, 2)
    for part, h in ((0, zh), (1, 1 - zh)):
        for i in (1, 2, 3):
            copy(cin(h), cin(h), cin_s.at[part, i - 1], cin_r.at[part, i - 1], dev()).wait_recv()
    grad(0, True)
    step(2, 2)
    grad(1)
    step(3, 2)
    grad(-1)
    through(2)
    through(-2)
    step(0, 3)
    owner(1)
    owner(-1)
    step(1, 3)
    grad(2)
    step(2, 3)
    grad(-2)
    step(3, 3)
    through(3)
    through(-3)
    owner(2)
    owner(-2)
    grad(3)
    grad(-3)
    for j in range(4):
        step(j, 4)
    through(4)
    owner(3)
    owner(-3)
    grad(4)

    def combined(kc):
        wf = Wb[kc].astype(F32)
        sgn = jnp.where(wf > 0, 1.0, jnp.where(wf < 0, -1.0, 0.0))
        return acc[0, kc] + sgn * acc[1, kc]

    wsend[...] = combined(ok)
    wg = copy(wsend, wrecv, sib_s.at[5], sib_r.at[5], sib)
    send(wg)
    ow[...] = combined(k)
    owner(4)
    wg.wait_recv()
    ow[...] = (ow[...] + wrecv[...]) * scale

    for yy in (0, 1):
        for h, kk in ((zh, ok), (1 - zh, k), (1 - zh, ok)):
            copy(Zs.at[0, 0], F.at[h, kk, yy], f_s.at[0], f_r.at[h, kk, yy], dev()).wait_recv()
    for a, o in ((0, oc), (1, orad)):
        for yy in (0, 1):
            for kk in (0, 1):
                gate = act[yy, pl.ds(kk * 32, 32)].astype(F32)
                o[yy, pl.ds(kk * 32, 32)] = gate * (F[0, kk, yy, a] + F[1, kk, yy, a])
    for c, cond in sent:
        if cond is None:
            c.wait_send()
        else:
            pl.when(cond)(c.wait_send)


def on_device(center, radius, grad_center, grad_radius, weight, active):
    vm = pl.BlockSpec(memory_space=pltpu.VMEM)
    dma = pltpu.SemaphoreType.DMA
    oc, orad, ow = pl.pallas_call(
        functools.partial(kernel, 2048.0 ** -0.5),
        out_shape=(
            jax.ShapeDtypeStruct((2, 64, 256), F32),
            jax.ShapeDtypeStruct((2, 64, 256), F32),
            jax.ShapeDtypeStruct((256, 512), F32),
        ),
        in_specs=[vm] * 6,
        out_specs=(vm,) * 3,
        scratch_shapes=[
            pltpu.VMEM((8, 2, 2, 128, 512), BF16),
            pltpu.VMEM((8, 2, 128, 256), BF16),
            pltpu.VMEM((2, 256, 512), BF16),
            pltpu.VMEM((2, 256, 512), BF16),
            pltpu.VMEM((8, 2, 2, 2, 32, 256), F32),
            pltpu.VMEM((4, 4, 2, 2, 32, 256), F32),
            pltpu.VMEM((4, 2, 2, 32, 256), F32),
            pltpu.VMEM((2, 2, 2, 2, 32, 256), F32),
            pltpu.VMEM((2, 2, 256, 512), F32),
            pltpu.VMEM((256, 512), F32),
            pltpu.VMEM((256, 512), F32),
            dma((2, 4, 4)), dma((2, 4, 4)),
            dma((2, 2)), dma((2, 2)),
            dma((2, 3)), dma((2, 3)),
            dma((6,)), dma((6,)),
            dma((3, 3)), dma((3, 3)),
            dma((8, 2)), dma((4, 4)),
            dma((6,)), dma((2, 2, 2)),
        ],
        compiler_params=pltpu.CompilerParams(collective_id=0, has_side_effects=True, vmem_limit_bytes=48 * 2**20),
        cost_estimate=pl.CostEstimate(flops=2 * 2**30, bytes_accessed=2**21, transcendentals=0),
        name="bounds",
    )(
        center.reshape(2, 64, 256), radius.reshape(2, 64, 256), grad_center, grad_radius, weight, active.reshape(2, 64, 256)
    )
    return oc.reshape(128, 256), orad.reshape(128, 256), ow


def solution(mesh):
    in_specs = (
        P("col", "row"),
        P("col", "row"),
        P("row", "col"),
        P("row", "col"),
        P("row", "col"),
        P("col", "row"),
    )
    out_specs = (P("col", "row"), P("col", "row"), P("row", "col"))
    return jax.shard_map(
        on_device, mesh=mesh, in_specs=in_specs, out_specs=out_specs, check_vma=False
    )
```

```python
import functools

import jax
import jax.numpy as jnp
from jax import lax
from jax.experimental import pallas as pl
from jax.experimental.pallas import tpu as pltpu
from jax.sharding import PartitionSpec as P

MESH = pl.DeviceIdType.MESH
F32 = jnp.float32
BF16 = jnp.bfloat16


def dot_nt(a, b):
    return lax.dot_general(a, b, (((1,), (1,)), ((), ())), preferred_element_type=F32)


def dot_tn(a, b):
    return lax.dot_general(a, b, (((0,), (0,)), ((), ())), preferred_element_type=F32)


def code(parts, out):
    ups = []
    for i, p in enumerate(parts):
        top = jnp.maximum(jnp.max(jnp.abs(p), axis=0, keepdims=True), 2.0 ** -100)
        e = jnp.floor(jnp.log2(top)) + 1.0
        q = jnp.clip(jnp.round(p * (jnp.exp2(-e) * 32767.0)), -32767.0, 32767.0)
        out[i * 32:(i + 1) * 32] = q.astype(jnp.int32).astype(jnp.int16)
        ups.append(jnp.broadcast_to(e.astype(jnp.int32), (16 // len(parts), 256)))
    out[len(parts) * 32:len(parts) * 32 + 16] = jnp.concatenate(ups, axis=0).astype(jnp.int16)


def decode(src, i, n):
    e = src[n * 32:n * 32 + 16].astype(jnp.int32)[i * (16 // n):i * (16 // n) + 1].astype(F32)
    return src[i * 32:(i + 1) * 32].astype(jnp.int32).astype(F32) * (jnp.exp2(e) * (1.0 / 32767.0))


def kernel(
    scale,
    ctr, rad, gc, gr, w, act,
    oc, orad, ow,
    G, C, Wb, Wa, S, R, Zs, F, acc, wsend, wrecv, gate,
    loc_s, ring_s, ring_r, own_s, own_r, z_s, z_r, sib_s, sib_r, cin_s, cin_r, x_s, x_r, f_s, f_r, ready,
):
    row, col = lax.axis_index("row"), lax.axis_index("col")
    zl, y = row // 8, row % 8
    zh, x, k = col // 8, (col % 8) // 2, col % 2
    z1, z0 = zl // 2, zl % 2
    mid = (z0 + z1) % 2
    ok, fz = 1 - k, 1 - zh
    up, down = (y + 1) % 8, (y + 7) % 8

    def dev(x=x, y=y, zl=zl, zh=zh, k=k):
        return (zl * 8 + y, zh * 8 + x * 2 + k)

    def flip(j):
        return ((z1 + j // 2) % 2) * 2 + (z0 + j % 2) % 2

    order = [0, 1, 2 + mid, 3 - mid]

    def z_of(pair, i):
        return pair * 2 + (z0 + i + mid * ((pair + z1) % 2)) % 2

    def rows32(i):
        return pl.ds(pl.multiple_of(i * 32, 32), 32)

    def rows64(i):
        return pl.ds(pl.multiple_of(i * 64, 64), 64)

    def at_y(off):
        return (y + off + 8) % 8

    sent = []

    def copy(src, dst, ssem, rsem, to):
        return pltpu.make_async_remote_copy(
            src_ref=src, dst_ref=dst, send_sem=ssem, recv_sem=rsem, device_id=to, device_id_type=MESH
        )

    def send(c, cond=None):
        if cond is None:
            c.start()
        else:
            pl.when(cond)(c.start)
        sent.append((c, cond))

    flying = [[], []]

    def send_y(c, i):
        c.start()
        flying[i].append(c)

    zrows = rows32(zl)
    cz = rows32(zh * 2 + x // 2)
    cy = (x % 2) * 4 + k * 2
    local = [
        pltpu.make_async_copy(src, dst, loc_s.at[i])
        for i, (src, dst) in enumerate((
            (gc.at[rows32(k)], G.at[y, 0, k, zrows]),
            (gr.at[rows32(k)], G.at[y, 1, k, zrows]),
            (w, Wb.at[k]),
            (ctr.at[:, rows32(k)], C.at[pl.ds(cy, 2), 0, cz]),
            (rad.at[:, rows32(k)], C.at[pl.ds(cy, 2), 1, cz]),
            (act, gate),
        ))
    ]
    for c in local:
        c.start()

    peers = [dev(y=up), dev(y=down), dev(k=ok)]
    peers += [dev(zl=flip(j)) for j in (1, 2, 3)]
    peers += [dev(x=(x + i) % 4, k=c) for i in (1, 2, 3) for c in (0, 1)]
    partner = dev(zh=fz)
    bar = pltpu.get_barrier_semaphore()
    for p in peers:
        pl.semaphore_signal(bar, inc=1, device_id=p, device_id_type=MESH)

    @pl.when(zh == 0)
    def _():
        pl.semaphore_signal(bar, inc=1, device_id=partner, device_id_type=MESH)
        pl.semaphore_wait(bar, len(peers))

    @pl.when(zh == 1)
    def _():
        pl.semaphore_wait(bar, len(peers) + 1)
        pl.semaphore_signal(ready, inc=1, device_id=partner, device_id_type=MESH)

    local[0].wait()
    local[1].wait()

    def own_y(part, kc):
        blk = G.at[y, :, kc, zrows]
        for i, to in enumerate((up, down)):
            send_y(copy(blk, blk, own_s.at[part, i], own_r.at[part, i], dev(y=to)), i)

    def own_z(part, kc):
        blk = G.at[y, :, kc, zrows]
        for i in (1, 2, 3):
            send(copy(blk, blk, z_s.at[part, i - 1], z_r.at[part, zl], dev(zl=flip(order[i]))))

    sib = dev(k=ok)
    gsib = [copy(ref.at[rows32(ok)], G.at[y, a, k, zrows], sib_s.at[a], sib_r.at[a], sib) for a, ref in enumerate((gc, gr))]
    csib = [
        copy(ref.at[:, rows32(ok)], C.at[pl.ds(cy, 2), a, cz], sib_s.at[2 + a], sib_r.at[2 + a], sib)
        for a, ref in enumerate((ctr, rad))
    ]
    wsib = copy(w, Wb.at[k], sib_s.at[4], sib_r.at[4], sib)
    for c in gsib:
        send(c)
    own_y(0, k)
    own_z(0, k)
    for c in gsib:
        c.wait_recv()
    own_y(1, ok)
    own_z(1, ok)
    for c in csib:
        send(c)
    send(wsib)

    def cin(h):
        return C.at[pl.ds((x % 2) * 4, 4), :, rows32(h * 2 + x // 2)]

    def cin_x(h, part):
        for i in (1, 2, 3):
            send(copy(cin(h), cin(h), cin_s.at[part, i - 1], cin_r.at[part, i - 1], dev(x=(x + i) % 4)))

    far = copy(cin(zh), cin(zh), cin_s.at[2, 0], cin_r.at[2, 0], partner)

    def ring_copy(zs, d, i):
        ys = at_y(d if i else -d)
        if d < 3:
            blk = G.at[ys, :, :, rows32(zs)]
        else:
            blk = G.at[ys, i, :, rows32(zs)]
        return copy(blk, blk, ring_s.at[i, d, zs], ring_r.at[i, d, zs], dev(y=down if i else up))

    def arrive(pair, i, d):
        zs = z_of(pair, i)
        if d == 0:
            for part in (0, 1):
                blk = G.at[y, :, k, rows32(zs)]
                copy(blk, blk, z_s.at[part, 0], z_r.at[part, zs], dev()).wait_recv()
        else:
            for j in (0, 1):
                ring_copy(zs, d - 1, j).wait_recv()

    def step(pair, i, d):
        arrive(pair, i, d)
        if d < 4:
            for j in (0, 1):
                send_y(ring_copy(z_of(pair, i), d, j), j)

    def x_copy(yb, h, g):
        xd, kd = g * 2 + yb // 4, (yb % 4) // 2
        c = copy(S.at[yb, h, g], R.at[x, k, yb % 2, h], x_s.at[yb, h, g], x_r.at[x, k, yb % 2, h], dev(x=xd, k=kd))
        return c, (xd == x) & (kd == k)

    def through(off, h):
        yb = at_y(off)
        p = [dot_nt(G[yb, a, 0, rows64(h)], m[0]) + dot_nt(G[yb, a, 1, rows64(h)], m[1]) for a, m in ((0, Wb), (1, Wa))]
        for g in (0, 1):
            code([t[g * 32:(g + 1) * 32] for t in p], S.at[yb, h, g])
        for g in (0, 1):
            c, here = x_copy(yb, h, g)
            send(c, jnp.logical_not(here))

            @pl.when(here)
            def _():
                R[x, k, yb % 2, h] = S[yb, h, g]

    def grad(blocks, first=False):
        for a in (0, 1):
            for kc in (0, 1):
                t = None
                for off, rows in blocks:
                    yb = at_y(off)
                    if rows is None:
                        p = dot_tn(C[yb, a], G[yb, a, kc])
                    else:
                        p = dot_tn(C[yb, a, rows64(rows)], G[yb, a, kc, rows64(rows)])
                    t = p if t is None else t + p
                if first:
                    acc[a, kc] = t
                else:
                    acc[a, kc] += t

    def arrived(h, yy):
        for i in range(4):
            for kk in (0, 1):
                xs = (x + i) % 4
                c = copy(S.at[0, 0, 0], R.at[xs, kk, yy, h], x_s.at[0, 0, 0], x_r.at[xs, kk, yy, h], dev())
                if i:
                    c.wait_recv()
                else:
                    pl.when(k != kk)(c.wait_recv)

    def total(h, yy, kk, a):
        r = [decode(R.at[i, kk, yy, h], a, 2) for i in range(4)]
        return (r[0] + r[1]) + (r[2] + r[3])

    def z_copy(yy):
        return copy(Zs.at[yy], F.at[yy], f_s.at[yy], f_r.at[yy], partner)

    P_, Q_ = z1, 1 - z1
    step(P_, 1, 0)
    def step_own():
        for part in (0, 1):
            for i in (0, 1):
                blk = G.at[y, :, k, zrows]
                copy(blk, blk, own_s.at[part, i], own_r.at[part, i], dev()).wait_recv()
        for j in (0, 1):
            send_y(ring_copy(zl, 1, j), j)

    step_own()
    step(Q_, 0, 0)
    step(P_, 1, 1)
    step(Q_, 1, 0)
    local[3].wait()
    local[4].wait()
    for c in csib:
        c.wait_recv()

    @pl.when(zh == 0)
    def _():
        pl.semaphore_wait(ready, 1)

    send(far)
    cin_x(zh, 0)
    local[2].wait()
    Wa[k] = jnp.abs(Wb[k])
    wsib.wait_recv()
    Wa[ok] = jnp.abs(Wb[ok])
    through(0, 0)
    through(0, 1)
    step(Q_, 0, 1)
    step(Q_, 1, 1)
    for off in (1, -1):
        for h in (0, 1):
            through(off, h)
    step(fz, 0, 2)
    step(fz, 1, 2)
    far_in = copy(cin(fz), cin(fz), cin_s.at[2, 0], cin_r.at[2, 0], dev())
    far_in.wait_recv()
    cin_x(fz, 1)
    through(2, fz)
    through(-2, fz)
    step(fz, 0, 3)
    step(fz, 1, 3)
    through(3, fz)
    through(-3, fz)
    step(zh, 0, 2)
    for part, h in ((0, zh), (1, fz)):
        for i in (1, 2, 3):
            copy(cin(h), cin(h), cin_s.at[part, i - 1], cin_r.at[part, i - 1], dev()).wait_recv()
    grad([(0, None)], True)
    step(fz, 0, 4)
    step(fz, 1, 4)
    through(4, fz)
    step(zh, 1, 2)
    through(2, zh)
    through(-2, zh)
    grad([(1, None), (-1, None)])
    step(zh, 0, 3)
    step(zh, 1, 3)
    through(3, zh)
    through(-3, zh)
    grad([(2, None), (-2, None)])
    for yy in (0, 1):
        arrived(fz, yy)
        code([total(fz, yy, kk, a) for kk in (0, 1) for a in (0, 1)], Zs.at[yy])
        send(z_copy(yy))
    grad([(3, None), (-3, None), (4, fz)])
    step(zh, 0, 4)
    step(zh, 1, 4)
    through(4, zh)
    grad([(4, zh)])

    def combined(kc):
        wf = Wb[kc].astype(F32)
        sgn = jnp.where(wf > 0, 1.0, jnp.where(wf < 0, -1.0, 0.0))
        return acc[0, kc] + sgn * acc[1, kc]

    wsend[...] = combined(ok)
    wg = copy(wsend, wrecv, sib_s.at[5], sib_r.at[5], sib)
    send(wg)
    ow[...] = combined(k)
    local[5].wait()
    for yy in (0, 1):
        z_copy(yy).wait_recv()
        arrived(zh, yy)
        for kk in (0, 1):
            rows = pl.ds(kk * 32, 32)
            g = gate[yy, rows].astype(F32)
            for a, o in ((0, oc), (1, orad)):
                o[yy, rows] = g * (total(zh, yy, kk, a) + decode(F.at[yy], kk * 2 + a, 4))
    wg.wait_recv()
    ow[...] = (ow[...] + wrecv[...]) * scale
    for c in flying[0] + flying[1]:
        c.wait_send()
    for c, cond in sent:
        if cond is None:
            c.wait_send()
        else:
            pl.when(cond)(c.wait_send)


def on_device(center, radius, grad_center, grad_radius, weight, active):
    hbm = pl.BlockSpec(memory_space=pl.ANY)
    vm = pl.BlockSpec(memory_space=pltpu.VMEM)
    dma = pltpu.SemaphoreType.DMA
    oc, orad, ow = pl.pallas_call(
        functools.partial(kernel, 2048.0 ** -0.5),
        out_shape=(
            jax.ShapeDtypeStruct((2, 64, 256), F32),
            jax.ShapeDtypeStruct((2, 64, 256), F32),
            jax.ShapeDtypeStruct((256, 512), F32),
        ),
        in_specs=[hbm] * 6,
        out_specs=(vm,) * 3,
        scratch_shapes=[
            pltpu.VMEM((8, 2, 2, 128, 512), BF16),
            pltpu.VMEM((8, 2, 128, 256), BF16),
            pltpu.VMEM((2, 256, 512), BF16),
            pltpu.VMEM((2, 256, 512), BF16),
            pltpu.VMEM((8, 2, 2, 80, 256), jnp.int16),
            pltpu.VMEM((4, 2, 2, 2, 80, 256), jnp.int16),
            pltpu.VMEM((2, 144, 256), jnp.int16),
            pltpu.VMEM((2, 144, 256), jnp.int16),
            pltpu.VMEM((2, 2, 256, 512), F32),
            pltpu.VMEM((256, 512), F32),
            pltpu.VMEM((256, 512), F32),
            pltpu.VMEM((2, 64, 256), jnp.int32),
            dma((6,)),
            dma((2, 4, 4)), dma((2, 4, 4)),
            dma((2, 2)), dma((2, 2)),
            dma((2, 3)), dma((2, 4)),
            dma((6,)), dma((6,)),
            dma((3, 3)), dma((3, 3)),
            dma((8, 2, 2)), dma((4, 2, 2, 2)),
            dma((2,)), dma((2,)),
            pltpu.SemaphoreType.REGULAR,
        ],
        compiler_params=pltpu.CompilerParams(collective_id=0, has_side_effects=True, vmem_limit_bytes=48 * 2**20),
        cost_estimate=pl.CostEstimate(flops=2 * 2**30, bytes_accessed=2**21, transcendentals=0),
        name="bounds",
    )(
        *[pltpu.with_memory_space_constraint(v, pltpu.HBM) for v in (
            center.reshape(2, 64, 256), radius.reshape(2, 64, 256), grad_center, grad_radius, weight, active.reshape(2, 64, 256)
        )]
    )
    return oc.reshape(128, 256), orad.reshape(128, 256), ow


def solution(mesh):
    in_specs = (
        P("col", "row"),
        P("col", "row"),
        P("row", "col"),
        P("row", "col"),
        P("row", "col"),
        P("col", "row"),
    )
    out_specs = (P("col", "row"), P("col", "row"), P("row", "col"))
    return jax.shard_map(
        on_device, mesh=mesh, in_specs=in_specs, out_specs=out_specs, check_vma=False
    )
```

```python
import functools

import jax
import jax.numpy as jnp
from jax import lax
from jax.experimental import pallas as pl
from jax.experimental.pallas import tpu as pltpu
from jax.sharding import PartitionSpec as P

MESH = pl.DeviceIdType.MESH
F32 = jnp.float32
BF16 = jnp.bfloat16


def dot_nt(a, b):
    return lax.dot_general(a, b, (((1,), (1,)), ((), ())), preferred_element_type=F32)


def dot_tn(a, b):
    return lax.dot_general(a, b, (((0,), (0,)), ((), ())), preferred_element_type=F32)


def code(parts, out):
    ups = []
    for i, p in enumerate(parts):
        top = jnp.maximum(jnp.max(jnp.abs(p), axis=0, keepdims=True), 2.0 ** -100)
        e = jnp.floor(jnp.log2(top)) + 1.0
        q = jnp.clip(jnp.round(p * (jnp.exp2(-e) * 32767.0)), -32767.0, 32767.0)
        out[i * 32:(i + 1) * 32] = q.astype(jnp.int32).astype(jnp.int16)
        ups.append(jnp.broadcast_to(e.astype(jnp.int32), (16 // len(parts), 256)))
    out[len(parts) * 32:len(parts) * 32 + 16] = jnp.concatenate(ups, axis=0).astype(jnp.int16)


def decode(src, i, n):
    e = src[n * 32:n * 32 + 16].astype(jnp.int32)[i * (16 // n):i * (16 // n) + 1].astype(F32)
    return src[i * 32:(i + 1) * 32].astype(jnp.int32).astype(F32) * (jnp.exp2(e) * (1.0 / 32767.0))


def kernel(
    scale,
    ctr, rad, gc, gr, w, act,
    oc, orad, ow,
    G, C, Wb, Wa, S, R, Zs, F, acc, wsend, wrecv, gate,
    loc_s, ring_s, ring_r, own_s, own_r, z_s, z_r, sib_s, sib_r, cin_s, cin_r, x_s, x_r, f_s, f_r, ready,
):
    row, col = lax.axis_index("row"), lax.axis_index("col")
    zl, y = row // 8, row % 8
    zh, x, k = col // 8, (col % 8) // 2, col % 2
    z1, z0 = zl // 2, zl % 2
    mid = (z0 + z1) % 2
    ok, fz = 1 - k, 1 - zh
    up, down = (y + 1) % 8, (y + 7) % 8

    def dev(x=x, y=y, zl=zl, zh=zh, k=k):
        return (zl * 8 + y, zh * 8 + x * 2 + k)

    def flip(j):
        return ((z1 + j // 2) % 2) * 2 + (z0 + j % 2) % 2

    order = [0, 1, 2 + mid, 3 - mid]

    def z_of(pair, i):
        return pair * 2 + (z0 + i + mid * ((pair + z1) % 2)) % 2

    def rows32(i):
        return pl.ds(pl.multiple_of(i * 32, 32), 32)

    def rows64(i):
        return pl.ds(pl.multiple_of(i * 64, 64), 64)

    def at_y(off):
        return (y + off + 8) % 8

    sent = []

    def copy(src, dst, ssem, rsem, to):
        return pltpu.make_async_remote_copy(
            src_ref=src, dst_ref=dst, send_sem=ssem, recv_sem=rsem, device_id=to, device_id_type=MESH
        )

    def send(c, cond=None):
        if cond is None:
            c.start()
        else:
            pl.when(cond)(c.start)
        sent.append((c, cond))

    flying = [[], []]

    def send_y(c, i):
        c.start()
        flying[i].append(c)

    zrows = rows32(zl)
    cz = rows32(zh * 2 + x // 2)
    cy = (x % 2) * 4 + k * 2
    local = [
        pltpu.make_async_copy(src, dst, loc_s.at[i])
        for i, (src, dst) in enumerate((
            (gc.at[rows32(k)], G.at[y, 0, k, zrows]),
            (gr.at[rows32(k)], G.at[y, 1, k, zrows]),
            (w, Wb.at[k]),
            (ctr.at[:, rows32(k)], C.at[pl.ds(cy, 2), 0, cz]),
            (rad.at[:, rows32(k)], C.at[pl.ds(cy, 2), 1, cz]),
            (act, gate),
        ))
    ]
    for c in local:
        c.start()

    peers = [dev(y=up), dev(y=down), dev(k=ok)]
    peers += [dev(zl=flip(j)) for j in (1, 2, 3)]
    peers += [dev(x=(x + i) % 4, k=c) for i in (1, 2, 3) for c in (0, 1)]
    partner = dev(zh=fz)
    bar = pltpu.get_barrier_semaphore()
    for p in peers:
        pl.semaphore_signal(bar, inc=1, device_id=p, device_id_type=MESH)

    @pl.when(zh == 0)
    def _():
        pl.semaphore_signal(bar, inc=1, device_id=partner, device_id_type=MESH)
        pl.semaphore_wait(bar, len(peers))

    @pl.when(zh == 1)
    def _():
        pl.semaphore_wait(bar, len(peers) + 1)
        pl.semaphore_signal(ready, inc=1, device_id=partner, device_id_type=MESH)

    local[0].wait()
    local[1].wait()

    def own_y(part, kc):
        blk = G.at[y, :, kc, zrows]
        for i, to in enumerate((up, down)):
            send_y(copy(blk, blk, own_s.at[part, i], own_r.at[part, i], dev(y=to)), i)

    def own_z(part, kc):
        blk = G.at[y, :, kc, zrows]
        for i in (1, 2, 3):
            send(copy(blk, blk, z_s.at[part, i - 1], z_r.at[part, zl], dev(zl=flip(order[i]))))

    sib = dev(k=ok)
    gsib = [copy(ref.at[rows32(ok)], G.at[y, a, k, zrows], sib_s.at[a], sib_r.at[a], sib) for a, ref in enumerate((gc, gr))]
    csib = [
        copy(ref.at[:, rows32(ok)], C.at[pl.ds(cy, 2), a, cz], sib_s.at[2 + a], sib_r.at[2 + a], sib)
        for a, ref in enumerate((ctr, rad))
    ]
    wsib = copy(w, Wb.at[k], sib_s.at[4], sib_r.at[4], sib)
    for c in gsib:
        send(c)
    own_y(0, k)
    own_z(0, k)
    for c in gsib:
        c.wait_recv()
    own_y(1, ok)
    own_z(1, ok)
    for c in csib:
        send(c)
    send(wsib)

    def cin(h):
        return C.at[pl.ds((x % 2) * 4, 4), :, rows32(h * 2 + x // 2)]

    def cin_x(h, part):
        for i in (1, 2, 3):
            send(copy(cin(h), cin(h), cin_s.at[part, i - 1], cin_r.at[part, i - 1], dev(x=(x + i) % 4)))

    far = copy(cin(zh), cin(zh), cin_s.at[2, 0], cin_r.at[2, 0], partner)

    def ring_copy(zs, d, i):
        ys = at_y(d if i else -d)
        if d < 3:
            blk = G.at[ys, :, :, rows32(zs)]
        else:
            blk = G.at[ys, i, :, rows32(zs)]
        return copy(blk, blk, ring_s.at[i, d, zs], ring_r.at[i, d, zs], dev(y=down if i else up))

    def arrive(pair, i, d):
        zs = z_of(pair, i)
        if d == 0:
            for part in (0, 1):
                blk = G.at[y, :, k, rows32(zs)]
                copy(blk, blk, z_s.at[part, 0], z_r.at[part, zs], dev()).wait_recv()
        else:
            for j in (0, 1):
                ring_copy(zs, d - 1, j).wait_recv()

    def step(pair, i, d):
        if d == 1 and i == 0:
            @pl.when(pair != z1)
            def _():
                arrive(pair, i, d)
                for j in (0, 1):
                    ring_copy(z_of(pair, i), d, j).start()

            for j in (0, 1):
                sent.append((ring_copy(z_of(pair, i), d, j), pair != z1))
            return
        arrive(pair, i, d)
        if d < 4:
            for j in (0, 1):
                send_y(ring_copy(z_of(pair, i), d, j), j)

    def x_copy(yb, h, g):
        xd, kd = g * 2 + yb // 4, (yb % 4) // 2
        c = copy(S.at[yb, h, g], R.at[x, k, yb % 2, h], x_s.at[yb, h, g], x_r.at[x, k, yb % 2, h], dev(x=xd, k=kd))
        return c, (xd == x) & (kd == k)

    def through(off, h):
        yb = at_y(off)
        p = [dot_nt(G[yb, a, 0, rows64(h)], m[0]) + dot_nt(G[yb, a, 1, rows64(h)], m[1]) for a, m in ((0, Wb), (1, Wa))]
        for g in (0, 1):
            code([t[g * 32:(g + 1) * 32] for t in p], S.at[yb, h, g])
        for g in (0, 1):
            c, here = x_copy(yb, h, g)
            send(c, jnp.logical_not(here))

            @pl.when(here)
            def _():
                R[x, k, yb % 2, h] = S[yb, h, g]

    def grad(blocks, first=False, columns=(0, 1)):
        for kc in columns:
            for a in (0, 1):
                t = None
                for off, rows in blocks:
                    yb = at_y(off)
                    if rows is None:
                        p = dot_tn(C[yb, a], G[yb, a, kc])
                    else:
                        p = dot_tn(C[yb, a, rows64(rows)], G[yb, a, kc, rows64(rows)])
                    t = p if t is None else t + p
                if first:
                    acc[a, kc] = t
                else:
                    acc[a, kc] += t

    def arrived(h, yy):
        for i in range(4):
            for kk in (0, 1):
                xs = (x + i) % 4
                c = copy(S.at[0, 0, 0], R.at[xs, kk, yy, h], x_s.at[0, 0, 0], x_r.at[xs, kk, yy, h], dev())
                if i:
                    c.wait_recv()
                else:
                    pl.when(k != kk)(c.wait_recv)

    def total(h, yy, kk, a):
        r = [decode(R.at[i, kk, yy, h], a, 2) for i in range(4)]
        return (r[0] + r[1]) + (r[2] + r[3])

    def z_copy(yy):
        return copy(Zs.at[yy], F.at[yy], f_s.at[yy], f_r.at[yy], partner)

    P_, Q_ = z1, 1 - z1

    def step_own():
        for part in (0, 1):
            for i in (0, 1):
                blk = G.at[y, :, k, zrows]
                copy(blk, blk, own_s.at[part, i], own_r.at[part, i], dev()).wait_recv()
        for j in (0, 1):
            send_y(ring_copy(zl, 1, j), j)

    step_own()
    step(P_, 1, 0)
    step(Q_, 0, 0)
    step(Q_, 1, 0)
    local[2].wait()
    Wa[k] = jnp.abs(Wb[k])
    wsib.wait_recv()
    Wa[ok] = jnp.abs(Wb[ok])
    through(0, 0)
    through(0, 1)
    def both(i, h):
        through(i, h)
        through(-i, h)

    step(fz, 0, 1)
    step(fz, 1, 1)
    local[3].wait()
    local[4].wait()
    for c in csib:
        c.wait_recv()

    @pl.when(zh == 0)
    def _():
        pl.semaphore_wait(ready, 1)

    send(far)
    cin_x(zh, 0)
    both(1, fz)
    step(fz, 0, 2)
    step(fz, 1, 2)
    both(2, fz)
    step(fz, 0, 3)
    step(fz, 1, 3)
    far_in = copy(cin(fz), cin(fz), cin_s.at[2, 0], cin_r.at[2, 0], dev())
    far_in.wait_recv()
    cin_x(fz, 1)
    both(3, fz)
    step(zh, 0, 1)
    step(zh, 1, 1)
    step(fz, 0, 4)
    step(fz, 1, 4)
    through(4, fz)
    both(1, zh)
    step(zh, 0, 2)
    step(zh, 1, 2)
    for yy in (0, 1):
        arrived(fz, yy)
        code([total(fz, yy, kk, a) for kk in (0, 1) for a in (0, 1)], Zs.at[yy])
        send(z_copy(yy))
    both(2, zh)
    for part, h in ((0, zh), (1, fz)):
        for i in (1, 2, 3):
            copy(cin(h), cin(h), cin_s.at[part, i - 1], cin_r.at[part, i - 1], dev()).wait_recv()
    grad([(0, None)], True)
    grad([(1, None), (-1, None)])
    step(zh, 0, 3)
    step(zh, 1, 3)
    both(3, zh)
    grad([(2, None), (-2, None)])
    grad([(3, None), (-3, None), (4, fz)])
    step(zh, 0, 4)
    step(zh, 1, 4)
    through(4, zh)

    def combined(kc):
        wf = Wb[kc].astype(F32)
        sgn = jnp.where(wf > 0, 1.0, jnp.where(wf < 0, -1.0, 0.0))
        return acc[0, kc] + sgn * acc[1, kc]

    grad([(4, zh)], columns=(ok,))
    wsend[...] = combined(ok)
    wg = copy(wsend, wrecv, sib_s.at[5], sib_r.at[5], sib)
    send(wg)
    grad([(4, zh)], columns=(k,))
    ow[...] = combined(k)
    local[5].wait()
    for yy in (0, 1):
        z_copy(yy).wait_recv()
        arrived(zh, yy)
        for kk in (0, 1):
            rows = pl.ds(kk * 32, 32)
            g = gate[yy, rows].astype(F32)
            for a, o in ((0, oc), (1, orad)):
                o[yy, rows] = g * (total(zh, yy, kk, a) + decode(F.at[yy], kk * 2 + a, 4))
    wg.wait_recv()
    ow[...] = (ow[...] + wrecv[...]) * scale
    for c in flying[0] + flying[1]:
        c.wait_send()
    for c, cond in sent:
        if cond is None:
            c.wait_send()
        else:
            pl.when(cond)(c.wait_send)


def on_device(center, radius, grad_center, grad_radius, weight, active):
    hbm = pl.BlockSpec(memory_space=pl.ANY)
    vm = pl.BlockSpec(memory_space=pltpu.VMEM)
    dma = pltpu.SemaphoreType.DMA
    oc, orad, ow = pl.pallas_call(
        functools.partial(kernel, 2048.0 ** -0.5),
        out_shape=(
            jax.ShapeDtypeStruct((2, 64, 256), F32),
            jax.ShapeDtypeStruct((2, 64, 256), F32),
            jax.ShapeDtypeStruct((256, 512), F32),
        ),
        in_specs=[hbm] * 6,
        out_specs=(vm,) * 3,
        scratch_shapes=[
            pltpu.VMEM((8, 2, 2, 128, 512), BF16),
            pltpu.VMEM((8, 2, 128, 256), BF16),
            pltpu.VMEM((2, 256, 512), BF16),
            pltpu.VMEM((2, 256, 512), BF16),
            pltpu.VMEM((8, 2, 2, 80, 256), jnp.int16),
            pltpu.VMEM((4, 2, 2, 2, 80, 256), jnp.int16),
            pltpu.VMEM((2, 144, 256), jnp.int16),
            pltpu.VMEM((2, 144, 256), jnp.int16),
            pltpu.VMEM((2, 2, 256, 512), F32),
            pltpu.VMEM((256, 512), F32),
            pltpu.VMEM((256, 512), F32),
            pltpu.VMEM((2, 64, 256), jnp.int32),
            dma((6,)),
            dma((2, 4, 4)), dma((2, 4, 4)),
            dma((2, 2)), dma((2, 2)),
            dma((2, 3)), dma((2, 4)),
            dma((6,)), dma((6,)),
            dma((3, 3)), dma((3, 3)),
            dma((8, 2, 2)), dma((4, 2, 2, 2)),
            dma((2,)), dma((2,)),
            pltpu.SemaphoreType.REGULAR,
        ],
        compiler_params=pltpu.CompilerParams(collective_id=0, has_side_effects=True, vmem_limit_bytes=48 * 2**20),
        cost_estimate=pl.CostEstimate(flops=2 * 2**30, bytes_accessed=2**21, transcendentals=0),
        name="bounds",
    )(
        *[pltpu.with_memory_space_constraint(v, pltpu.HBM) for v in (
            center.reshape(2, 64, 256), radius.reshape(2, 64, 256), grad_center, grad_radius, weight, active.reshape(2, 64, 256)
        )]
    )
    return oc.reshape(128, 256), orad.reshape(128, 256), ow


def solution(mesh):
    in_specs = (
        P("col", "row"),
        P("col", "row"),
        P("row", "col"),
        P("row", "col"),
        P("row", "col"),
        P("col", "row"),
    )
    out_specs = (P("col", "row"), P("col", "row"), P("row", "col"))
    return jax.shard_map(
        on_device, mesh=mesh, in_specs=in_specs, out_specs=out_specs, check_vma=False
    )
```

```python
import functools

import jax
import jax.numpy as jnp
from jax import lax
from jax.experimental import pallas as pl
from jax.experimental.pallas import tpu as pltpu
from jax.sharding import PartitionSpec as P

MESH = pl.DeviceIdType.MESH
F32 = jnp.float32
BF16 = jnp.bfloat16


def dot_nt(a, b):
    return lax.dot_general(a, b, (((1,), (1,)), ((), ())), preferred_element_type=F32)


def dot_tn(a, b):
    return lax.dot_general(a, b, (((0,), (0,)), ((), ())), preferred_element_type=F32)


def code(parts, out):
    ups = []
    for i, p in enumerate(parts):
        top = jnp.maximum(jnp.max(jnp.abs(p), axis=0, keepdims=True), 2.0 ** -100)
        e = jnp.floor(jnp.log2(top)) + 1.0
        q = jnp.clip(jnp.round(p * (jnp.exp2(-e) * 32767.0)), -32767.0, 32767.0)
        out[i * 32:(i + 1) * 32] = q.astype(jnp.int32).astype(jnp.int16)
        ups.append(jnp.broadcast_to(e.astype(jnp.int32), (16 // len(parts), 256)))
    out[len(parts) * 32:len(parts) * 32 + 16] = jnp.concatenate(ups, axis=0).astype(jnp.int16)


def decode(src, i, n):
    e = src[n * 32:n * 32 + 16].astype(jnp.int32)[i * (16 // n):i * (16 // n) + 1].astype(F32)
    return src[i * 32:(i + 1) * 32].astype(jnp.int32).astype(F32) * (jnp.exp2(e) * (1.0 / 32767.0))


def kernel(
    scale,
    ctr, rad, gc, gr, w, act,
    oc, orad, ow,
    G, C, Wb, Wa, S, R, Zs, F, acc, wsend, wrecv, gate,
    loc_s, ring_s, ring_r, own_s, own_r, z_s, z_r, sib_s, sib_r, cin_s, cin_r, x_s, x_r, f_s, f_r, ready,
):
    row, col = lax.axis_index("row"), lax.axis_index("col")
    zl, y = row // 8, row % 8
    zh, x, k = col // 8, (col % 8) // 2, col % 2
    z1, z0 = zl // 2, zl % 2
    mid = (z0 + z1) % 2
    ok, fz = 1 - k, 1 - zh
    up, down = (y + 1) % 8, (y + 7) % 8

    def dev(x=x, y=y, zl=zl, zh=zh, k=k):
        return (zl * 8 + y, zh * 8 + x * 2 + k)

    def flip(j):
        return ((z1 + j // 2) % 2) * 2 + (z0 + j % 2) % 2

    order = [0, 1, 2 + mid, 3 - mid]

    def z_of(pair, i):
        return pair * 2 + (z0 + i + mid * ((pair + z1) % 2)) % 2

    def rows32(i):
        return pl.ds(pl.multiple_of(i * 32, 32), 32)

    def rows64(i):
        return pl.ds(pl.multiple_of(i * 64, 64), 64)

    def at_y(off):
        return (y + off + 8) % 8

    sent = []

    def copy(src, dst, ssem, rsem, to):
        return pltpu.make_async_remote_copy(
            src_ref=src, dst_ref=dst, send_sem=ssem, recv_sem=rsem, device_id=to, device_id_type=MESH
        )

    def send(c, cond=None):
        if cond is None:
            c.start()
        else:
            pl.when(cond)(c.start)
        sent.append((c, cond))

    flying = [[], []]

    def send_y(c, i):
        c.start()
        flying[i].append(c)

    zrows = rows32(zl)
    cz = rows32(zh * 2 + x // 2)
    cy = (x % 2) * 4 + k * 2
    local = [
        pltpu.make_async_copy(src, dst, loc_s.at[i])
        for i, (src, dst) in enumerate((
            (gc.at[rows32(k)], G.at[y, 0, k, zrows]),
            (gr.at[rows32(k)], G.at[y, 1, k, zrows]),
            (w, Wb.at[k]),
            (ctr.at[:, rows32(k)], C.at[pl.ds(cy, 2), 0, cz]),
            (rad.at[:, rows32(k)], C.at[pl.ds(cy, 2), 1, cz]),
            (act, gate),
        ))
    ]
    for c in local:
        c.start()

    peers = [dev(y=up), dev(y=down), dev(k=ok)]
    peers += [dev(zl=flip(j)) for j in (1, 2, 3)]
    peers += [dev(x=(x + i) % 4, k=c) for i in (1, 2, 3) for c in (0, 1)]
    partner = dev(zh=fz)
    bar = pltpu.get_barrier_semaphore()
    for p in peers:
        pl.semaphore_signal(bar, inc=1, device_id=p, device_id_type=MESH)

    @pl.when(zh == 0)
    def _():
        pl.semaphore_signal(bar, inc=1, device_id=partner, device_id_type=MESH)
        pl.semaphore_wait(bar, len(peers))

    @pl.when(zh == 1)
    def _():
        pl.semaphore_wait(bar, len(peers) + 1)
        pl.semaphore_signal(ready, inc=1, device_id=partner, device_id_type=MESH)

    local[0].wait()
    local[1].wait()

    def own_y(part, kc):
        blk = G.at[y, :, kc, zrows]
        for i, to in enumerate((up, down)):
            send_y(copy(blk, blk, own_s.at[part, i], own_r.at[part, i], dev(y=to)), i)

    def own_z(part, kc):
        blk = G.at[y, :, kc, zrows]
        for i in (1, 2, 3):
            send(copy(blk, blk, z_s.at[part, i - 1], z_r.at[part, zl], dev(zl=flip(order[i]))))

    sib = dev(k=ok)
    gsib = [copy(ref.at[rows32(ok)], G.at[y, a, k, zrows], sib_s.at[a], sib_r.at[a], sib) for a, ref in enumerate((gc, gr))]
    csib = [
        copy(ref.at[:, rows32(ok)], C.at[pl.ds(cy, 2), a, cz], sib_s.at[2 + a], sib_r.at[2 + a], sib)
        for a, ref in enumerate((ctr, rad))
    ]
    wsib = copy(w, Wb.at[k], sib_s.at[4], sib_r.at[4], sib)
    for c in gsib:
        send(c)
    own_y(0, k)
    own_z(0, k)
    for c in gsib:
        c.wait_recv()
    own_y(1, ok)
    own_z(1, ok)
    for c in csib:
        send(c)
    send(wsib)

    def cin(h):
        return C.at[pl.ds((x % 2) * 4, 4), :, rows32(h * 2 + x // 2)]

    def cin_x(h, part):
        for i in (1, 2, 3):
            send(copy(cin(h), cin(h), cin_s.at[part, i - 1], cin_r.at[part, i - 1], dev(x=(x + i) % 4)))

    far = copy(cin(zh), cin(zh), cin_s.at[2, 0], cin_r.at[2, 0], partner)

    def ring_copy(zs, d, i, part):
        ys = at_y(d if i else -d)
        kc = ok if part else k
        blk = G.at[ys, :, kc, rows32(zs)] if d < 3 else G.at[ys, i, kc, rows32(zs)]
        return copy(blk, blk, ring_s.at[i, d, zs, part], ring_r.at[i, d, zs, part], dev(y=down if i else up))

    def arrive(zs, d, j, part):
        if d == 0:
            blk = G.at[y, :, k, rows32(zs)]
            copy(blk, blk, z_s.at[part, 0], z_r.at[part, zs], dev()).wait_recv()
        else:
            ring_copy(zs, d - 1, j, part).wait_recv()

    def pass_on(zs, d):
        for part in (0, 1):
            if d == 0:
                arrive(zs, 0, 0, part)
            for j in (0, 1):
                if d:
                    arrive(zs, d, j, part)
                if d < 4:
                    ring_copy(zs, d, j, part).start()

    def step(pair, i, d):
        zs = z_of(pair, i)
        cond = None
        if d == 1 and i == 0:
            cond = pair != z1
            pl.when(cond)(lambda: pass_on(zs, d))
        else:
            pass_on(zs, d)
        if d < 4:
            for part in (0, 1):
                for j in (0, 1):
                    sent.append((ring_copy(zs, d, j, part), cond))

    def x_copy(yb, h, g):
        xd, kd = g * 2 + yb // 4, (yb % 4) // 2
        c = copy(S.at[yb, h, g], R.at[x, k, yb % 2, h], x_s.at[yb, h, g], x_r.at[x, k, yb % 2, h], dev(x=xd, k=kd))
        return c, (xd == x) & (kd == k)

    def through(off, h):
        yb = at_y(off)
        p = [dot_nt(G[yb, a, 0, rows64(h)], m[0]) + dot_nt(G[yb, a, 1, rows64(h)], m[1]) for a, m in ((0, Wb), (1, Wa))]
        for g in (0, 1):
            code([t[g * 32:(g + 1) * 32] for t in p], S.at[yb, h, g])
        for g in (0, 1):
            c, here = x_copy(yb, h, g)
            send(c, jnp.logical_not(here))

            @pl.when(here)
            def _():
                R[x, k, yb % 2, h] = S[yb, h, g]

    def through_last():
        yb = at_y(4)
        for i in (0, 1):
            step(zh, i, 4)
            zs = z_of(zh, i)
            g = zs % 2
            p = [dot_nt(G[yb, a, 0, rows32(zs)], m[0]) + dot_nt(G[yb, a, 1, rows32(zs)], m[1]) for a, m in ((0, Wb), (1, Wa))]
            code(p, S.at[yb, zh, g])
            c, here = x_copy(yb, zh, g)
            send(c, jnp.logical_not(here))

            @pl.when(here)
            def _():
                R[x, k, yb % 2, zh] = S[yb, zh, g]

    def grad(blocks, first=False, columns=(0, 1)):
        for kc in columns:
            for a in (0, 1):
                t = None
                for off, rows in blocks:
                    yb = at_y(off)
                    if rows is None:
                        p = dot_tn(C[yb, a], G[yb, a, kc])
                    else:
                        p = dot_tn(C[yb, a, rows64(rows)], G[yb, a, kc, rows64(rows)])
                    t = p if t is None else t + p
                if first:
                    acc[a, kc] = t
                else:
                    acc[a, kc] += t

    def arrived(h, yy):
        for i in range(4):
            for kk in (0, 1):
                xs = (x + i) % 4
                c = copy(S.at[0, 0, 0], R.at[xs, kk, yy, h], x_s.at[0, 0, 0], x_r.at[xs, kk, yy, h], dev())
                if i:
                    c.wait_recv()
                else:
                    pl.when(k != kk)(c.wait_recv)

    def total(h, yy, kk, a):
        r = [decode(R.at[i, kk, yy, h], a, 2) for i in range(4)]
        return (r[0] + r[1]) + (r[2] + r[3])

    def z_copy(yy):
        return copy(Zs.at[yy], F.at[yy], f_s.at[yy], f_r.at[yy], partner)

    P_, Q_ = z1, 1 - z1

    def step_own():
        blk = G.at[y, :, k, zrows]
        for part in (0, 1):
            for j in (0, 1):
                copy(blk, blk, own_s.at[part, j], own_r.at[part, j], dev()).wait_recv()
                send_y(ring_copy(zl, 1, j, part), j)

    step_own()
    step(P_, 1, 0)
    step(Q_, 0, 0)
    step(Q_, 1, 0)
    local[2].wait()
    Wa[k] = jnp.abs(Wb[k])
    wsib.wait_recv()
    Wa[ok] = jnp.abs(Wb[ok])
    through(0, 0)
    through(0, 1)
    def both(i, h):
        through(i, h)
        through(-i, h)

    step(fz, 0, 1)
    step(fz, 1, 1)
    local[3].wait()
    local[4].wait()
    for c in csib:
        c.wait_recv()

    @pl.when(zh == 0)
    def _():
        pl.semaphore_wait(ready, 1)

    send(far)
    cin_x(zh, 0)
    both(1, fz)
    step(fz, 0, 2)
    step(fz, 1, 2)
    both(2, fz)
    step(fz, 0, 3)
    step(fz, 1, 3)
    far_in = copy(cin(fz), cin(fz), cin_s.at[2, 0], cin_r.at[2, 0], dev())
    far_in.wait_recv()
    cin_x(fz, 1)
    both(3, fz)
    step(zh, 0, 1)
    step(zh, 1, 1)
    step(fz, 0, 4)
    step(fz, 1, 4)
    through(4, fz)
    both(1, zh)
    step(zh, 0, 2)
    step(zh, 1, 2)
    for yy in (0, 1):
        arrived(fz, yy)
        code([total(fz, yy, kk, a) for kk in (0, 1) for a in (0, 1)], Zs.at[yy])
        send(z_copy(yy))
    both(2, zh)
    for part, h in ((0, zh), (1, fz)):
        for i in (1, 2, 3):
            copy(cin(h), cin(h), cin_s.at[part, i - 1], cin_r.at[part, i - 1], dev()).wait_recv()
    grad([(0, None)], True)
    grad([(1, None), (-1, None)])
    step(zh, 0, 3)
    step(zh, 1, 3)
    both(3, zh)
    grad([(2, None), (-2, None)])
    grad([(3, None), (-3, None), (4, fz)])
    through_last()

    def combined(kc):
        wf = Wb[kc].astype(F32)
        sgn = jnp.where(wf > 0, 1.0, jnp.where(wf < 0, -1.0, 0.0))
        return acc[0, kc] + sgn * acc[1, kc]

    grad([(4, zh)], columns=(ok,))
    wsend[...] = combined(ok)
    wg = copy(wsend, wrecv, sib_s.at[5], sib_r.at[5], sib)
    send(wg)
    grad([(4, zh)], columns=(k,))
    ow[...] = combined(k)
    local[5].wait()
    for yy in (0, 1):
        z_copy(yy).wait_recv()
        arrived(zh, yy)
        for kk in (0, 1):
            rows = pl.ds(kk * 32, 32)
            g = gate[yy, rows].astype(F32)
            for a, o in ((0, oc), (1, orad)):
                o[yy, rows] = g * (total(zh, yy, kk, a) + decode(F.at[yy], kk * 2 + a, 4))
    wg.wait_recv()
    ow[...] = (ow[...] + wrecv[...]) * scale
    for c in flying[0] + flying[1]:
        c.wait_send()
    for c, cond in sent:
        if cond is None:
            c.wait_send()
        else:
            pl.when(cond)(c.wait_send)


def on_device(center, radius, grad_center, grad_radius, weight, active):
    hbm = pl.BlockSpec(memory_space=pl.ANY)
    vm = pl.BlockSpec(memory_space=pltpu.VMEM)
    dma = pltpu.SemaphoreType.DMA
    oc, orad, ow = pl.pallas_call(
        functools.partial(kernel, 2048.0 ** -0.5),
        out_shape=(
            jax.ShapeDtypeStruct((2, 64, 256), F32),
            jax.ShapeDtypeStruct((2, 64, 256), F32),
            jax.ShapeDtypeStruct((256, 512), F32),
        ),
        in_specs=[hbm] * 6,
        out_specs=(vm,) * 3,
        scratch_shapes=[
            pltpu.VMEM((8, 2, 2, 128, 512), BF16),
            pltpu.VMEM((8, 2, 128, 256), BF16),
            pltpu.VMEM((2, 256, 512), BF16),
            pltpu.VMEM((2, 256, 512), BF16),
            pltpu.VMEM((8, 2, 2, 80, 256), jnp.int16),
            pltpu.VMEM((4, 2, 2, 2, 80, 256), jnp.int16),
            pltpu.VMEM((2, 144, 256), jnp.int16),
            pltpu.VMEM((2, 144, 256), jnp.int16),
            pltpu.VMEM((2, 2, 256, 512), F32),
            pltpu.VMEM((256, 512), F32),
            pltpu.VMEM((256, 512), F32),
            pltpu.VMEM((2, 64, 256), jnp.int32),
            dma((6,)),
            dma((2, 4, 4, 2)), dma((2, 4, 4, 2)),
            dma((2, 2)), dma((2, 2)),
            dma((2, 3)), dma((2, 4)),
            dma((6,)), dma((6,)),
            dma((3, 3)), dma((3, 3)),
            dma((8, 2, 2)), dma((4, 2, 2, 2)),
            dma((2,)), dma((2,)),
            pltpu.SemaphoreType.REGULAR,
        ],
        compiler_params=pltpu.CompilerParams(collective_id=0, has_side_effects=True, vmem_limit_bytes=48 * 2**20),
        cost_estimate=pl.CostEstimate(flops=2 * 2**30, bytes_accessed=2**21, transcendentals=0),
        name="bounds",
    )(
        *[pltpu.with_memory_space_constraint(v, pltpu.HBM) for v in (
            center.reshape(2, 64, 256), radius.reshape(2, 64, 256), grad_center, grad_radius, weight, active.reshape(2, 64, 256)
        )]
    )
    return oc.reshape(128, 256), orad.reshape(128, 256), ow


def solution(mesh):
    in_specs = (
        P("col", "row"),
        P("col", "row"),
        P("row", "col"),
        P("row", "col"),
        P("row", "col"),
        P("col", "row"),
    )
    out_specs = (P("col", "row"), P("col", "row"), P("row", "col"))
    return jax.shard_map(
        on_device, mesh=mesh, in_specs=in_specs, out_specs=out_specs, check_vma=False
    )
```

```python
import functools

import jax
import jax.numpy as jnp
from jax import lax
from jax.experimental import pallas as pl
from jax.experimental.pallas import tpu as pltpu
from jax.sharding import PartitionSpec as P

MESH = pl.DeviceIdType.MESH
F32 = jnp.float32
BF16 = jnp.bfloat16


def dot_nt(a, b):
    return lax.dot_general(a, b, (((1,), (1,)), ((), ())), preferred_element_type=F32)


def dot_tn(a, b):
    return lax.dot_general(a, b, (((0,), (0,)), ((), ())), preferred_element_type=F32)


def code(parts, out):
    ups = []
    for i, p in enumerate(parts):
        top = jnp.maximum(jnp.max(jnp.abs(p), axis=0, keepdims=True), 2.0 ** -100)
        e = jnp.floor(jnp.log2(top)) + 1.0
        q = jnp.clip(jnp.round(p * (jnp.exp2(-e) * 32767.0)), -32767.0, 32767.0)
        out[i * 32:(i + 1) * 32] = q.astype(jnp.int32).astype(jnp.int16)
        ups.append(jnp.broadcast_to(e.astype(jnp.int32), (16 // len(parts), 256)))
    out[len(parts) * 32:len(parts) * 32 + 16] = jnp.concatenate(ups, axis=0).astype(jnp.int16)


def decode(src, i, n):
    e = src[n * 32:n * 32 + 16].astype(jnp.int32)[i * (16 // n):i * (16 // n) + 1].astype(F32)
    return src[i * 32:(i + 1) * 32].astype(jnp.int32).astype(F32) * (jnp.exp2(e) * (1.0 / 32767.0))


def kernel(
    scale,
    ctr, rad, gc, gr, w, act,
    oc, orad, ow,
    G, C, Wb, Wa, S, R, Zs, F, acc, wsend, wrecv, gate,
    loc_s, ring_s, ring_r, own_s, own_r, z_s, z_r, sib_s, sib_r, cin_s, cin_r, x_s, x_r, f_s, f_r, ready,
):
    row, col = lax.axis_index("row"), lax.axis_index("col")
    zl, y = row // 8, row % 8
    zh, x, k = col // 8, (col % 8) // 2, col % 2
    z1, z0 = zl // 2, zl % 2
    mid = (z0 + z1) % 2
    ok, fz = 1 - k, 1 - zh
    up, down = (y + 1) % 8, (y + 7) % 8

    def dev(x=x, y=y, zl=zl, zh=zh, k=k):
        return (zl * 8 + y, zh * 8 + x * 2 + k)

    def flip(j):
        return ((z1 + j // 2) % 2) * 2 + (z0 + j % 2) % 2

    order = [0, 1, 2 + mid, 3 - mid]

    def z_of(pair, i):
        return pair * 2 + (z0 + i + mid * ((pair + z1) % 2)) % 2

    def rows32(i):
        return pl.ds(pl.multiple_of(i * 32, 32), 32)

    def rows64(i):
        return pl.ds(pl.multiple_of(i * 64, 64), 64)

    def at_y(off):
        return (y + off + 8) % 8

    sent = []

    def copy(src, dst, ssem, rsem, to):
        return pltpu.make_async_remote_copy(
            src_ref=src, dst_ref=dst, send_sem=ssem, recv_sem=rsem, device_id=to, device_id_type=MESH
        )

    def send(c, cond=None):
        if cond is None:
            c.start()
        else:
            pl.when(cond)(c.start)
        sent.append((c, cond))

    flying = [[], []]

    def send_y(c, i):
        c.start()
        flying[i].append(c)

    zrows = rows32(zl)
    cz = rows32(zh * 2 + x // 2)
    cy = (x % 2) * 4 + k * 2
    local = [
        pltpu.make_async_copy(src, dst, loc_s.at[i])
        for i, (src, dst) in enumerate((
            (gc.at[rows32(k)], G.at[y, 0, k, zrows]),
            (gr.at[rows32(k)], G.at[y, 1, k, zrows]),
            (w, Wb.at[k]),
            (ctr.at[:, rows32(k)], C.at[pl.ds(cy, 2), 0, cz]),
            (rad.at[:, rows32(k)], C.at[pl.ds(cy, 2), 1, cz]),
            (act, gate),
        ))
    ]
    for c in local:
        c.start()

    peers = [dev(y=up), dev(y=down), dev(k=ok)]
    peers += [dev(zl=flip(j)) for j in (1, 2, 3)]
    peers += [dev(x=(x + i) % 4, k=c) for i in (1, 2, 3) for c in (0, 1)]
    partner = dev(zh=fz)
    bar = pltpu.get_barrier_semaphore()
    for p in peers:
        pl.semaphore_signal(bar, inc=1, device_id=p, device_id_type=MESH)

    @pl.when(zh == 0)
    def _():
        pl.semaphore_signal(bar, inc=1, device_id=partner, device_id_type=MESH)
        pl.semaphore_wait(bar, len(peers))

    @pl.when(zh == 1)
    def _():
        pl.semaphore_wait(bar, len(peers) + 1)
        pl.semaphore_signal(ready, inc=1, device_id=partner, device_id_type=MESH)

    local[0].wait()
    local[1].wait()

    def own_y(part, kc):
        blk = G.at[y, :, kc, zrows]
        for i, to in enumerate((up, down)):
            send_y(copy(blk, blk, own_s.at[part, i], own_r.at[part, i], dev(y=to)), i)

    def own_z(part, kc):
        blk = G.at[y, :, kc, zrows]
        for i in (1, 2, 3):
            send(copy(blk, blk, z_s.at[part, i - 1], z_r.at[part, zl], dev(zl=flip(order[i]))))

    sib = dev(k=ok)
    gsib = [copy(ref.at[rows32(ok)], G.at[y, a, k, zrows], sib_s.at[a], sib_r.at[a], sib) for a, ref in enumerate((gc, gr))]
    csib = [
        copy(ref.at[:, rows32(ok)], C.at[pl.ds(cy, 2), a, cz], sib_s.at[2 + a], sib_r.at[2 + a], sib)
        for a, ref in enumerate((ctr, rad))
    ]
    wsib = copy(w, Wb.at[k], sib_s.at[4], sib_r.at[4], sib)
    for c in gsib:
        send(c)
    own_y(0, k)
    own_z(0, k)
    for c in gsib:
        c.wait_recv()
    own_y(1, ok)
    own_z(1, ok)
    for c in csib:
        send(c)
    send(wsib)

    def cin(h):
        return C.at[pl.ds((x % 2) * 4, 4), :, rows32(h * 2 + x // 2)]

    def cin_x(h, part):
        for i in (1, 2, 3):
            send(copy(cin(h), cin(h), cin_s.at[part, i - 1], cin_r.at[part, i - 1], dev(x=(x + i) % 4)))

    far = copy(cin(zh), cin(zh), cin_s.at[2, 0], cin_r.at[2, 0], partner)

    def ring_copy(zs, d, i, part):
        ys = at_y(d if i else -d)
        kc = ok if part else k
        blk = G.at[ys, :, kc, rows32(zs)] if d < 3 else G.at[ys, i, kc, rows32(zs)]
        return copy(blk, blk, ring_s.at[i, d, zs, part], ring_r.at[i, d, zs, part], dev(y=down if i else up))

    def arrive(zs, d, j, part):
        if d == 0:
            blk = G.at[y, :, k, rows32(zs)]
            copy(blk, blk, z_s.at[part, 0], z_r.at[part, zs], dev()).wait_recv()
        else:
            ring_copy(zs, d - 1, j, part).wait_recv()

    def pass_on(zs, d):
        for part in (0, 1):
            if d == 0:
                arrive(zs, 0, 0, part)
            for j in (0, 1):
                if d:
                    arrive(zs, d, j, part)
                if d < 4:
                    ring_copy(zs, d, j, part).start()

    def step(pair, i, d):
        zs = z_of(pair, i)
        cond = None
        if d == 1 and i == 0:
            cond = pair != z1
            pl.when(cond)(lambda: pass_on(zs, d))
        else:
            pass_on(zs, d)
        if d < 4:
            for part in (0, 1):
                for j in (0, 1):
                    sent.append((ring_copy(zs, d, j, part), cond))

    def x_copy(yb, h, g):
        xd, kd = g * 2 + yb // 4, (yb % 4) // 2
        c = copy(S.at[yb, h, g], R.at[x, k, yb % 2, h], x_s.at[yb, h, g], x_r.at[x, k, yb % 2, h], dev(x=xd, k=kd))
        return c, (xd == x) & (kd == k)

    def through(off, h):
        yb = at_y(off)
        p = [dot_nt(G[yb, a, 0, rows64(h)], m[0]) + dot_nt(G[yb, a, 1, rows64(h)], m[1]) for a, m in ((0, Wb), (1, Wa))]
        for g in (0, 1):
            code([t[g * 32:(g + 1) * 32] for t in p], S.at[yb, h, g])
        for g in (0, 1):
            c, here = x_copy(yb, h, g)
            send(c, jnp.logical_not(here))

            @pl.when(here)
            def _():
                R[x, k, yb % 2, h] = S[yb, h, g]

    def through_last():
        yb = at_y(4)
        for i in (0, 1):
            step(zh, i, 4)
            zs = z_of(zh, i)
            g = zs % 2
            p = [dot_nt(G[yb, a, 0, rows32(zs)], m[0]) + dot_nt(G[yb, a, 1, rows32(zs)], m[1]) for a, m in ((0, Wb), (1, Wa))]
            code(p, S.at[yb, zh, g])
            c, here = x_copy(yb, zh, g)
            send(c, jnp.logical_not(here))

            @pl.when(here)
            def _():
                R[x, k, yb % 2, zh] = S[yb, zh, g]

    def grad(blocks, first=False, columns=(0, 1)):
        for kc in columns:
            for a in (0, 1):
                t = None
                for off, rows in blocks:
                    yb = at_y(off)
                    if rows is None:
                        p = dot_tn(C[yb, a], G[yb, a, kc])
                    else:
                        p = dot_tn(C[yb, a, rows64(rows)], G[yb, a, kc, rows64(rows)])
                    t = p if t is None else t + p
                if first:
                    acc[a, kc] = t
                else:
                    acc[a, kc] += t

    def arrived(h, yy):
        for i in range(4):
            for kk in (0, 1):
                xs = (x + i) % 4
                c = copy(S.at[0, 0, 0], R.at[xs, kk, yy, h], x_s.at[0, 0, 0], x_r.at[xs, kk, yy, h], dev())
                if i:
                    c.wait_recv()
                else:
                    pl.when(k != kk)(c.wait_recv)

    def total(h, yy, kk, a):
        r = [decode(R.at[i, kk, yy, h], a, 2) for i in range(4)]
        return (r[0] + r[1]) + (r[2] + r[3])

    def z_copy(yy):
        return copy(Zs.at[yy], F.at[yy], f_s.at[yy], f_r.at[yy], partner)

    P_, Q_ = z1, 1 - z1

    def step_own():
        blk = G.at[y, :, k, zrows]
        for part in (0, 1):
            for j in (0, 1):
                copy(blk, blk, own_s.at[part, j], own_r.at[part, j], dev()).wait_recv()
                send_y(ring_copy(zl, 1, j, part), j)

    step_own()
    step(P_, 1, 0)
    step(Q_, 0, 0)
    step(Q_, 1, 0)
    local[2].wait()
    Wa[k] = jnp.abs(Wb[k])
    wsib.wait_recv()
    Wa[ok] = jnp.abs(Wb[ok])
    def both(i, h):
        through(i, h)
        through(-i, h)

    step(fz, 0, 1)
    step(fz, 1, 1)
    local[3].wait()
    local[4].wait()
    for c in csib:
        c.wait_recv()

    @pl.when(zh == 0)
    def _():
        pl.semaphore_wait(ready, 1)

    send(far)
    cin_x(zh, 0)
    through(0, fz)
    both(1, fz)
    step(fz, 0, 2)
    step(fz, 1, 2)
    both(2, fz)
    step(zh, 0, 1)
    step(fz, 0, 3)
    step(fz, 1, 3)
    far_in = copy(cin(fz), cin(fz), cin_s.at[2, 0], cin_r.at[2, 0], dev())
    far_in.wait_recv()
    cin_x(fz, 1)
    both(3, fz)
    step(zh, 1, 1)
    step(fz, 0, 4)
    step(fz, 1, 4)
    through(4, fz)
    through(0, zh)
    both(1, zh)
    step(zh, 0, 2)
    step(zh, 1, 2)
    for yy in (0, 1):
        arrived(fz, yy)
        code([total(fz, yy, kk, a) for kk in (0, 1) for a in (0, 1)], Zs.at[yy])
        send(z_copy(yy))
    both(2, zh)
    for part, h in ((0, zh), (1, fz)):
        for i in (1, 2, 3):
            copy(cin(h), cin(h), cin_s.at[part, i - 1], cin_r.at[part, i - 1], dev()).wait_recv()
    grad([(0, None)], True)
    grad([(1, None), (-1, None)])
    step(zh, 0, 3)
    step(zh, 1, 3)
    both(3, zh)
    grad([(2, None), (-2, None)])
    grad([(3, None), (-3, None), (4, fz)])
    through_last()

    def combined(kc):
        wf = Wb[kc].astype(F32)
        sgn = jnp.where(wf > 0, 1.0, jnp.where(wf < 0, -1.0, 0.0))
        return acc[0, kc] + sgn * acc[1, kc]

    grad([(4, zh)], columns=(ok,))
    wsend[...] = combined(ok)
    wg = copy(wsend, wrecv, sib_s.at[5], sib_r.at[5], sib)
    send(wg)
    grad([(4, zh)], columns=(k,))
    ow[...] = combined(k)
    local[5].wait()
    for yy in (0, 1):
        z_copy(yy).wait_recv()
        arrived(zh, yy)
        for kk in (0, 1):
            rows = pl.ds(kk * 32, 32)
            g = gate[yy, rows].astype(F32)
            for a, o in ((0, oc), (1, orad)):
                o[yy, rows] = g * (total(zh, yy, kk, a) + decode(F.at[yy], kk * 2 + a, 4))
    wg.wait_recv()
    ow[...] = (ow[...] + wrecv[...]) * scale
    for c in flying[0] + flying[1]:
        c.wait_send()
    for c, cond in sent:
        if cond is None:
            c.wait_send()
        else:
            pl.when(cond)(c.wait_send)


def on_device(center, radius, grad_center, grad_radius, weight, active):
    hbm = pl.BlockSpec(memory_space=pl.ANY)
    vm = pl.BlockSpec(memory_space=pltpu.VMEM)
    dma = pltpu.SemaphoreType.DMA
    oc, orad, ow = pl.pallas_call(
        functools.partial(kernel, 2048.0 ** -0.5),
        out_shape=(
            jax.ShapeDtypeStruct((2, 64, 256), F32),
            jax.ShapeDtypeStruct((2, 64, 256), F32),
            jax.ShapeDtypeStruct((256, 512), F32),
        ),
        in_specs=[hbm] * 6,
        out_specs=(vm,) * 3,
        scratch_shapes=[
            pltpu.VMEM((8, 2, 2, 128, 512), BF16),
            pltpu.VMEM((8, 2, 128, 256), BF16),
            pltpu.VMEM((2, 256, 512), BF16),
            pltpu.VMEM((2, 256, 512), BF16),
            pltpu.VMEM((8, 2, 2, 80, 256), jnp.int16),
            pltpu.VMEM((4, 2, 2, 2, 80, 256), jnp.int16),
            pltpu.VMEM((2, 144, 256), jnp.int16),
            pltpu.VMEM((2, 144, 256), jnp.int16),
            pltpu.VMEM((2, 2, 256, 512), F32),
            pltpu.VMEM((256, 512), F32),
            pltpu.VMEM((256, 512), F32),
            pltpu.VMEM((2, 64, 256), jnp.int32),
            dma((6,)),
            dma((2, 4, 4, 2)), dma((2, 4, 4, 2)),
            dma((2, 2)), dma((2, 2)),
            dma((2, 3)), dma((2, 4)),
            dma((6,)), dma((6,)),
            dma((3, 3)), dma((3, 3)),
            dma((8, 2, 2)), dma((4, 2, 2, 2)),
            dma((2,)), dma((2,)),
            pltpu.SemaphoreType.REGULAR,
        ],
        compiler_params=pltpu.CompilerParams(collective_id=0, has_side_effects=True, vmem_limit_bytes=48 * 2**20),
        cost_estimate=pl.CostEstimate(flops=2 * 2**30, bytes_accessed=2**21, transcendentals=0),
        name="bounds",
    )(
        *[pltpu.with_memory_space_constraint(v, pltpu.HBM) for v in (
            center.reshape(2, 64, 256), radius.reshape(2, 64, 256), grad_center, grad_radius, weight, active.reshape(2, 64, 256)
        )]
    )
    return oc.reshape(128, 256), orad.reshape(128, 256), ow


def solution(mesh):
    in_specs = (
        P("col", "row"),
        P("col", "row"),
        P("row", "col"),
        P("row", "col"),
        P("row", "col"),
        P("col", "row"),
    )
    out_specs = (P("col", "row"), P("col", "row"), P("row", "col"))
    return jax.shard_map(
        on_device, mesh=mesh, in_specs=in_specs, out_specs=out_specs, check_vma=False
    )
```
